32 devices in a mesh: groups: 2 (over y), docs: 4 (over z), proj: 4 (over x, core).
Axes of the slice: x: 2, y: 2, z: 4, core: 2. Of those that a mesh axis runs over, the one named last changes fastest.
Arguments:
- queries: bfloat16 [1216, 65536], P(('groups', 'docs'), 'proj'), parts along dimension 0, may hold values from -6 to 6
- store: bfloat16 [1280, 65536], P(('groups', 'docs'), 'proj'), parts along dimension 0, may hold values from -0.0234375 to 0.0234375
Outputs:
- scores: float32 [608, 1280], P('proj', ('groups', 'docs')), parts along dimension 1
The draws below stay inside these ranges and needn't reach their ends.
There are 2 independent parts, one for each index of `groups`. The reference program is written for one: setup_inputs(seed, part) draws one part's arguments, and reference() takes and returns one part's arrays. A program takes and returns all parts, laid end to end along the dimension named above; each array names one. Nothing has to cross between parts.
All inputs are finite; a program needn't handle non-finite values.
Results may differ from the reference program's by a relative error of at most 0.0003.
Values may be sent and summed in bfloat16 or wider, within the bound.
No kernel may reach another device: no remote copies, remote signals or barrier semaphores. Data moves between devices by JAX's collectives and lax.ppermute only.
A program may use at most 64 MiB of HBM per device.

```python
import jax
import jax.numpy as jnp
from jax import lax

P_SIZE = 65536
Q_DEV = 152
DOCS_DEV = 160
WIN = 4
NQ = 608
NDOCS = 640


def block_levels(rng, extent, shards, least, largest):
    factor_of = 1.0
    for position, parts in shards:
        heights = jax.random.uniform(jax.random.fold_in(jax.random.fold_in(rng, 6), position), (parts,), jnp.float32, least / len(shards), largest / len(shards))
        factor_of = factor_of * jnp.repeat(jnp.exp(heights), extent[position] // parts).reshape((-1,) + (1,) * (len(extent) - 1 - position))
    return factor_of


def centred(stream_key, extent, spread, limit, split=(), dtype=jnp.bfloat16):
    level = block_levels(stream_key, extent, split, -0.22, 0.18) if split else 1.0
    result = jax.random.normal(stream_key, extent, jnp.float32) * spread * level
    return jnp.minimum(jnp.maximum(result, -limit), limit).astype(dtype)


def setup_inputs(seed: int = 0, part: int = 0) -> dict:
    keys = jax.random.split(jax.random.key(seed), 3)
    own_keys = jax.random.split(jax.random.fold_in(keys[2], part), 3)
    queries = centred(own_keys[0], (NQ, P_SIZE), 1.0, 6.0, ((0, 4), (1, 4)))
    store = centred(own_keys[1], (NDOCS, P_SIZE), P_SIZE ** -0.5, 0.0234375, ((0, 4), (1, 4)))
    return dict(queries=queries, store=store)


def reference(queries, store):
    blocks = NQ // Q_DEV
    query_blocks = queries.reshape(blocks, Q_DEV, P_SIZE)
    store_blocks = store.reshape(blocks, DOCS_DEV, P_SIZE)
    tiles = []
    for k in range(WIN):
        rolled = jnp.roll(query_blocks, -k, axis=0)

        def one_shard(pair):
            return lax.dot_general(pair[0], pair[1], (((1,), (1,)), ((), ())), preferred_element_type=jnp.float32)

        shard_scores = lax.map(one_shard, (rolled, store_blocks))
        tiles.append(jnp.transpose(shard_scores, (1, 0, 2)).reshape(Q_DEV, NDOCS))
    return jnp.concatenate(tiles, axis=0)
```

```python
import jax
import jax.numpy as jnp
from jax import lax
from jax.sharding import PartitionSpec as P

WINDOW = 4
LINE = 4


def from_behind(value, axis, steps):
    count = lax.axis_size(axis)
    pairs = [(source, (source + steps) % count) for source in range(count)]
    return lax.ppermute(value, axis, pairs)


def products(rows, docs):
    return lax.dot_general(
        rows, docs, (((1,), (1,)), ((), ())), preferred_element_type=jnp.float32
    )


def ring(queries, store):
    blocks = [queries]
    for _ in range(WINDOW - 1):
        blocks.append(from_behind(blocks[-1], "docs", -1))
    return lax.psum_scatter(
        products(jnp.concatenate(blocks, axis=0), store),
        "proj",
        scatter_dimension=0,
        tiled=True,
    )


def after(value, *others):
    return lax.optimization_barrier((value,) + others)[0]


ENDS = [(0, 1), (1, 0), (2, 3), (3, 2)]
MIDDLE = [(1, 2), (2, 1)]
OUTWARD = [(1, 0), (2, 3)]
INWARD = [(0, 1), (3, 2)]
CORES = [(0, 1), (1, 0), (2, 3), (3, 2)]
CHIPS = [(0, 2), (1, 3), (2, 0), (3, 1)]


def along(value, pairs):
    return lax.ppermute(value, "docs", pairs)


def line(queries, store):
    depth = queries.shape[1]
    cut = depth // 4 // 128 * 128
    last = depth * 7 // 8 // 128 * 128
    place = lax.axis_index("docs")
    share = lax.axis_index("proj")
    inner = (place == 1) | (place == 2)
    left = place < 2
    near_store, far_store = store[:, :cut], store[:, cut:]

    middle = along(queries, MIDDLE)
    ends_near = along(queries[:, :cut], ENDS)
    ends_rest = along(after(queries[:, cut:], ends_near), ENDS)
    far_near = along(ends_near, MIDDLE)
    ends_held = after(ends_rest, middle)
    far_body = along(ends_held[:, : last - cut], MIDDLE)
    relayed = along(middle[:, :cut], OUTWARD)
    outer_store = along(after(far_store, ends_rest), INWARD)
    far_relayed = along(after(far_near, relayed), OUTWARD)
    far_tail = along(after(ends_rest[:, last - cut :], far_relayed), MIDDLE)

    own_part = products(queries, store)
    ends_part = products(ends_near, near_store) + products(ends_rest, far_store)
    middle_part = products(middle, store) + products(relayed, near_store)
    far_part = (
        products(far_near, near_store)
        + products(far_relayed, near_store)
        + products(far_body, store[:, cut:last])
        + products(far_tail, store[:, last:])
    )
    help_middle = products(middle[:, cut:], outer_store)
    help_far = products(far_body, outer_store[:, : last - cut]) + products(far_tail, outer_store[:, last - cut :])

    first = own_part
    second = jnp.where(inner & left, middle_part, jnp.where(inner, ends_part, jnp.where(left, ends_part, far_part)))
    third = jnp.where(inner, far_part, middle_part)
    fourth = jnp.where(inner, jnp.where(left, ends_part, middle_part), jnp.where(left, far_part, ends_part))
    return first, second, third, fourth, help_middle, help_far, inner, left, share


def finish(first, second, third, fourth, help_middle, help_far, inner, left, share):
    even = share % 2 == 0
    low = share < 2
    rows = first.shape[0]
    kept = jnp.concatenate([jnp.where(even, first, second), jnp.where(even, third, fourth), jnp.where(even, help_middle, help_far)], axis=0)
    given = jnp.concatenate([jnp.where(even, second, first), jnp.where(even, fourth, third), jnp.where(even, help_far, help_middle)], axis=0)
    total = kept + lax.ppermute(given, "proj", CORES)
    below, above, helped = total[:rows], total[rows : 2 * rows], total[2 * rows :]
    def at(docs, proj):
        return docs * 4 + proj

    one = [
        (at(1, 0), at(0, 2)), (at(1, 1), at(0, 3)),
        (at(2, 0), at(3, 2)), (at(2, 1), at(3, 1)),
    ]
    two = [
        (at(1, 2), at(0, 2)), (at(1, 3), at(0, 3)),
        (at(2, 2), at(3, 2)), (at(2, 3), at(3, 1)),
    ]
    over = lax.ppermute(jnp.where(low, above, below), "proj", CHIPS)
    help_one = lax.ppermute(helped, ("docs", "proj"), one)
    help_two = lax.ppermute(helped, ("docs", "proj"), two)
    return jnp.where(low, below, above) + over + help_one + help_two


def per_device(queries, store):
    if lax.axis_size("docs") == LINE and lax.axis_size("proj") == WINDOW:
        return finish(*line(queries, store))
    return ring(queries, store)


def solution(mesh):
    placed = (P(("groups", "docs"), "proj"), P(("groups", "docs"), "proj"))
    return jax.shard_map(
        per_device,
        mesh=mesh,
        in_specs=placed,
        out_specs=P("proj", ("groups", "docs")),
        check_vma=False,
    )
```

```python
import jax
import jax.numpy as jnp
from jax import lax
from jax.sharding import PartitionSpec as P

WINDOW = 4
LINE = 4


def from_behind(value, axis, steps):
    count = lax.axis_size(axis)
    pairs = [(source, (source + steps) % count) for source in range(count)]
    return lax.ppermute(value, axis, pairs)


def products(rows, docs):
    return lax.dot_general(
        rows, docs, (((1,), (1,)), ((), ())), preferred_element_type=jnp.float32
    )


def ring(queries, store):
    blocks = [queries]
    for _ in range(WINDOW - 1):
        blocks.append(from_behind(blocks[-1], "docs", -1))
    return lax.psum_scatter(
        products(jnp.concatenate(blocks, axis=0), store),
        "proj",
        scatter_dimension=0,
        tiled=True,
    )


def after(value, *others):
    return lax.optimization_barrier((value,) + others)[0]


ENDS = [(0, 1), (1, 0), (2, 3), (3, 2)]
MIDDLE = [(1, 2), (2, 1)]
OUTWARD = [(1, 0), (2, 3)]
INWARD = [(0, 1), (3, 2)]
CORES = [(0, 1), (1, 0), (2, 3), (3, 2)]
CHIPS = [(0, 2), (1, 3), (2, 0), (3, 1)]


def along(value, pairs):
    return lax.ppermute(value, "docs", pairs)


def across(value, pairs):
    parts = lax.axis_size("proj")
    return lax.ppermute(
        value, ("docs", "proj"), [(a * parts + b, c * parts + d) for a, b, c, d in pairs]
    )


def line(queries, store):
    depth = queries.shape[1]
    cut = depth * 11 // 32 // 128 * 128
    start = depth // 16 // 128 * 128
    last = depth * 13 // 16 // 128 * 128 - cut
    first, body, tail = slice(0, start), slice(start, last), slice(last, None)
    place = lax.axis_index("docs")
    share = lax.axis_index("proj")
    inner = (place == 1) | (place == 2)
    left = place < 2
    even = share % 2 == 0
    low = share < 2
    near_store, far_store = store[:, :cut], store[:, cut:]

    middle = along(queries, MIDDLE)
    ends_near = along(queries[:, :cut], ENDS)
    ends_rest = along(after(queries[:, cut:], ends_near, far_store), ENDS)
    far_near = along(ends_near, MIDDLE)
    relayed = along(middle[:, :cut], OUTWARD)
    far_first = along(after(ends_rest[:, first], middle), MIDDLE)
    outer_store = along(after(far_store, middle), INWARD)
    far_body = along(after(ends_rest[:, body], middle), MIDDLE)
    far_relayed = along(after(far_near, relayed, far_first), OUTWARD)
    far_tail = along(after(ends_rest[:, tail], far_relayed, far_first), MIDDLE)

    own_part = products(queries, store)
    ends_part = products(ends_near, near_store) + products(ends_rest, far_store)
    middle_part = products(middle, store) + products(relayed, near_store)
    zeros = jnp.zeros_like(own_part)
    second = jnp.where(inner & left, middle_part, jnp.where(inner | left, ends_part, zeros))
    third = jnp.where(inner, zeros, middle_part)
    fourth = jnp.where(left, jnp.where(inner, ends_part, zeros), jnp.where(inner, middle_part, ends_part))
    kept = jnp.concatenate([jnp.where(even, own_part, second), jnp.where(even, third, fourth)], axis=0)
    given = jnp.concatenate([jnp.where(even, second, own_part), jnp.where(even, fourth, third)], axis=0)
    kept = kept + lax.ppermute(given, "proj", CORES)
    rows = queries.shape[0]
    early = jnp.where(low, kept[:rows], kept[rows:]) + lax.ppermute(
        jnp.where(low, kept[rows:], kept[:rows]), "proj", CHIPS
    )

    helped = products(middle[:, cut:], outer_store)
    helped = helped + lax.ppermute(helped, "proj", [(1, 0), (3, 2)])
    helped_one = across(helped, [(1, 0, 0, 2), (2, 0, 3, 2)])
    helped_two = across(helped, [(1, 2, 0, 2), (2, 2, 3, 2)])

    far_body = after(far_body, far_relayed)
    for_inner = (
        products(far_near, near_store)
        + products(far_first, far_store[:, first])
        + products(far_body, far_store[:, body])
    )
    for_outer = (
        products(far_relayed, near_store)
        + products(far_first, outer_store[:, first])
        + products(far_body, outer_store[:, body])
    )
    kept = jnp.where(even, for_inner, for_outer)
    given = jnp.where(even, for_outer, for_inner)
    kept_store = jnp.where(even, far_store[:, tail], outer_store[:, tail])
    given_store = jnp.where(even, outer_store[:, tail], far_store[:, tail])
    kept, given, kept_store, given_store, early, helped_one, helped_two = lax.optimization_barrier(
        (kept, given, kept_store, given_store, early, helped_one, helped_two)
    )
    given = given + products(far_tail, given_store)
    kept = kept + products(far_tail, kept_store)
    kept = kept + lax.ppermute(given, "proj", CORES)
    one = across(kept, [(1, 0, 1, 2), (2, 0, 2, 2), (1, 1, 0, 3), (2, 3, 3, 1)])
    two = across(kept, [(1, 3, 0, 3), (2, 1, 3, 1)])
    three = across(kept, [(0, 1, 0, 3), (3, 3, 3, 1)])
    stays = jnp.where(share == jnp.where(inner, 2, jnp.where(left, 3, 1)), kept, 0.0)
    return early + helped_one + helped_two + stays + one + two + three


def per_device(queries, store):
    if lax.axis_size("docs") == LINE and lax.axis_size("proj") == WINDOW:
        return line(queries, store)
    return ring(queries, store)


def solution(mesh):
    placed = (P(("groups", "docs"), "proj"), P(("groups", "docs"), "proj"))
    return jax.shard_map(
        per_device,
        mesh=mesh,
        in_specs=placed,
        out_specs=P("proj", ("groups", "docs")),
        check_vma=False,
    )
```

```python
import jax
import jax.numpy as jnp
from jax import lax
from jax.sharding import PartitionSpec as P

WINDOW = 4
LINE = 4


def from_behind(value, axis, steps):
    count = lax.axis_size(axis)
    pairs = [(source, (source + steps) % count) for source in range(count)]
    return lax.ppermute(value, axis, pairs)


def products(rows, docs):
    return lax.dot_general(
        rows, docs, (((1,), (1,)), ((), ())), preferred_element_type=jnp.float32
    )


def ring(queries, store):
    blocks = [queries]
    for _ in range(WINDOW - 1):
        blocks.append(from_behind(blocks[-1], "docs", -1))
    return lax.psum_scatter(
        products(jnp.concatenate(blocks, axis=0), store),
        "proj",
        scatter_dimension=0,
        tiled=True,
    )


def after(value, *others):
    return lax.optimization_barrier((value,) + others)[0]


ENDS = [(0, 1), (1, 0), (2, 3), (3, 2)]
MIDDLE = [(1, 2), (2, 1)]
OUTWARD = [(1, 0), (2, 3)]
INWARD = [(0, 1), (3, 2)]
CORES = [(0, 1), (1, 0), (2, 3), (3, 2)]
CHIPS = [(0, 2), (1, 3), (2, 0), (3, 1)]


def along(value, pairs):
    return lax.ppermute(value, "docs", pairs)


def across(value, pairs):
    parts = lax.axis_size("proj")
    return lax.ppermute(
        value, ("docs", "proj"), [(a * parts + b, c * parts + d) for a, b, c, d in pairs]
    )


def line(queries, store):
    depth = queries.shape[1]
    cut = depth * 11 // 32 // 128 * 128
    start = depth // 16 // 128 * 128
    last = depth * 13 // 16 // 128 * 128 - cut
    first, body, tail = slice(0, start), slice(start, last), slice(last, None)
    place = lax.axis_index("docs")
    share = lax.axis_index("proj")
    inner = (place == 1) | (place == 2)
    left = place < 2
    even = share % 2 == 0
    low = share < 2
    near_store, far_store = store[:, :cut], store[:, cut:]

    middle = along(queries, MIDDLE)
    ends_near = along(queries[:, :cut], ENDS)
    ends_rest = along(after(queries[:, cut:], ends_near, far_store), ENDS)
    far_near = along(ends_near, MIDDLE)
    relayed = along(middle[:, :cut], OUTWARD)
    far_first = along(after(ends_rest[:, first], middle), MIDDLE)
    outer_store = along(after(far_store, middle), INWARD)
    far_body = along(after(ends_rest[:, body], middle), MIDDLE)
    far_relayed = along(after(far_near, relayed, far_first), OUTWARD)
    far_tail = along(after(ends_rest[:, tail], far_relayed, far_first), MIDDLE)

    own_part = products(queries, store)
    ends_part = products(ends_near, near_store) + products(ends_rest, far_store)
    middle_part = products(middle, store) + products(relayed, near_store)
    zeros = jnp.zeros_like(own_part)
    second = jnp.where(inner & left, middle_part, jnp.where(inner | left, ends_part, zeros))
    third = jnp.where(inner, zeros, middle_part)
    fourth = jnp.where(left, jnp.where(inner, ends_part, zeros), jnp.where(inner, middle_part, ends_part))
    kept = jnp.concatenate([jnp.where(even, own_part, second), jnp.where(even, third, fourth)], axis=0)
    given = jnp.concatenate([jnp.where(even, second, own_part), jnp.where(even, fourth, third)], axis=0)
    kept = kept + lax.ppermute(given, "proj", CORES)
    rows = queries.shape[0]
    early = jnp.where(low, kept[:rows], kept[rows:]) + lax.ppermute(
        jnp.where(low, kept[rows:], kept[:rows]), "proj", CHIPS
    )

    helped = products(middle[:, cut:], outer_store)
    helped = helped + lax.ppermute(helped, "proj", [(1, 0), (3, 2)])
    helped_one = across(helped, [(1, 0, 0, 2), (2, 0, 3, 2)])
    helped_two = across(helped, [(1, 2, 0, 2), (2, 2, 3, 2)])

    for_inner = products(far_near, near_store) + products(far_first, far_store[:, first])
    for_outer = products(far_relayed, near_store)
    kept_store = jnp.where(even, far_store[:, tail], outer_store[:, tail])
    given_store = jnp.where(even, outer_store[:, tail], far_store[:, tail])
    far_body, for_inner, for_outer, kept_store, given_store = lax.optimization_barrier(
        (far_body, for_inner, for_outer, kept_store, given_store, helped)
    )[:5]
    for_inner = for_inner + products(far_body, far_store[:, body])
    for_outer = (
        for_outer
        + products(far_first, outer_store[:, first])
        + products(far_body, outer_store[:, body])
    )
    kept = jnp.where(even, for_inner, for_outer)
    given = jnp.where(even, for_outer, for_inner)
    kept, given, kept_store, given_store, early = lax.optimization_barrier(
        (kept, given, kept_store, given_store, early)
    )
    given = given + products(far_tail, given_store)
    kept = kept + products(far_tail, kept_store)
    kept = kept + lax.ppermute(given, "proj", CORES)
    one = across(kept, [(1, 0, 1, 2), (2, 0, 2, 2), (1, 1, 0, 3), (2, 3, 3, 1)])
    two = across(kept, [(1, 3, 0, 3), (2, 1, 3, 1)])
    three = across(kept, [(0, 1, 0, 3), (3, 3, 3, 1)])
    stays = jnp.where(share == jnp.where(inner, 2, jnp.where(left, 3, 1)), kept, 0.0)
    return early + helped_one + helped_two + stays + one + two + three


def per_device(queries, store):
    if lax.axis_size("docs") == LINE and lax.axis_size("proj") == WINDOW:
        return line(queries, store)
    return ring(queries, store)


def solution(mesh):
    placed = (P(("groups", "docs"), "proj"), P(("groups", "docs"), "proj"))
    return jax.shard_map(
        per_device,
        mesh=mesh,
        in_specs=placed,
        out_specs=P("proj", ("groups", "docs")),
        check_vma=False,
    )
```

```python
import jax
import jax.numpy as jnp
from jax import lax
from jax.sharding import PartitionSpec as P

WINDOW = 4
LINE = 4


def from_behind(value, axis, steps):
    count = lax.axis_size(axis)
    pairs = [(source, (source + steps) % count) for source in range(count)]
    return lax.ppermute(value, axis, pairs)


def products(rows, docs):
    return lax.dot_general(
        rows, docs, (((1,), (1,)), ((), ())), preferred_element_type=jnp.float32
    )


def ring(queries, store):
    blocks = [queries]
    for _ in range(WINDOW - 1):
        blocks.append(from_behind(blocks[-1], "docs", -1))
    return lax.psum_scatter(
        products(jnp.concatenate(blocks, axis=0), store),
        "proj",
        scatter_dimension=0,
        tiled=True,
    )


def after(value, *others):
    return lax.optimization_barrier((value,) + others)[0]


ENDS = [(0, 1), (1, 0), (2, 3), (3, 2)]
MIDDLE = [(1, 2), (2, 1)]
OUTWARD = [(1, 0), (2, 3)]
INWARD = [(0, 1), (3, 2)]
CORES = [(0, 1), (1, 0), (2, 3), (3, 2)]
CHIPS = [(0, 2), (1, 3), (2, 0), (3, 1)]


def along(value, pairs):
    return lax.ppermute(value, "docs", pairs)


def across(value, pairs):
    parts = lax.axis_size("proj")
    return lax.ppermute(
        value, ("docs", "proj"), [(a * parts + b, c * parts + d) for a, b, c, d in pairs]
    )


def line(queries, store):
    depth = queries.shape[1]
    cut = depth * 11 // 32 // 128 * 128
    last = depth * 13 // 16 // 128 * 128 - cut
    body, tail = slice(0, last), slice(last, None)
    place = lax.axis_index("docs")
    share = lax.axis_index("proj")
    inner = (place == 1) | (place == 2)
    left = place < 2
    even = share % 2 == 0
    low = share < 2
    near_store, far_store = store[:, :cut], store[:, cut:]

    middle = along(queries, MIDDLE)
    ends_near = along(queries[:, :cut], ENDS)
    ends_rest = along(after(queries[:, cut:], ends_near, far_store), ENDS)
    far_near = along(ends_near, MIDDLE)
    relayed = along(middle[:, :cut], OUTWARD)
    outer_store = along(after(far_store, middle), INWARD)
    far_body = along(after(ends_rest[:, body], middle), MIDDLE)
    far_relayed = along(after(far_near, relayed), OUTWARD)
    far_tail = along(after(ends_rest[:, tail], far_relayed), MIDDLE)

    own_part = products(queries, store)
    ends_part = products(ends_near, near_store) + products(ends_rest, far_store)
    middle_part = products(middle, store) + products(relayed, near_store)
    zeros = jnp.zeros_like(own_part)
    second = jnp.where(inner & left, middle_part, jnp.where(inner | left, ends_part, zeros))
    third = jnp.where(inner, zeros, middle_part)
    fourth = jnp.where(left, jnp.where(inner, ends_part, zeros), jnp.where(inner, middle_part, ends_part))
    kept = jnp.concatenate([jnp.where(even, own_part, second), jnp.where(even, third, fourth)], axis=0)
    given = jnp.concatenate([jnp.where(even, second, own_part), jnp.where(even, fourth, third)], axis=0)
    kept = kept + lax.ppermute(given, "proj", CORES)
    rows = queries.shape[0]
    early = jnp.where(low, kept[:rows], kept[rows:]) + lax.ppermute(
        jnp.where(low, kept[rows:], kept[:rows]), "proj", CHIPS
    )

    helped = products(middle[:, cut:], outer_store) + products(far_relayed, near_store)
    helped = helped + across(
        helped,
        [(z, p + odd, z, p + 1 - odd) for z, odd in [(0, 0), (1, 1), (2, 1), (3, 0)] for p in (0, 2)],
    )
    helped_one = across(helped, [(1, 0, 0, 2), (2, 0, 3, 2), (0, 1, 0, 3), (3, 3, 3, 1)])
    helped_two = across(helped, [(1, 2, 0, 2), (2, 2, 3, 2)])
    helped_stays = jnp.where(~inner & (share == jnp.where(left, 3, 1)), helped, 0.0)
    early = early + helped_one + helped_two + helped_stays

    far_part = products(far_near, near_store)
    kept_store = jnp.where(even, far_store[:, tail], outer_store[:, tail])
    given_store = jnp.where(even, outer_store[:, tail], far_store[:, tail])
    far_body, far_part, kept_store, given_store, helped = lax.optimization_barrier(
        (far_body, far_part, kept_store, given_store, helped)
    )
    far_part = far_part + products(far_body, far_store[:, body])
    outer_part = products(far_body, outer_store[:, body])
    kept = jnp.where(even, far_part, outer_part)
    given = jnp.where(even, outer_part, far_part)
    kept, given, kept_store, given_store, early = lax.optimization_barrier(
        (kept, given, kept_store, given_store, early)
    )
    given = given + products(far_tail, given_store)
    kept = kept + products(far_tail, kept_store)
    kept = kept + lax.ppermute(given, "proj", CORES)
    two = across(kept, [(1, 3, 0, 3), (2, 1, 3, 1)])
    one = across(kept, [(1, 0, 1, 2), (2, 0, 2, 2), (1, 1, 0, 3), (2, 3, 3, 1)])
    return early + jnp.where(inner & (share == 2), kept, 0.0) + one + two


def per_device(queries, store):
    if lax.axis_size("docs") == LINE and lax.axis_size("proj") == WINDOW:
        return line(queries, store)
    return ring(queries, store)


def solution(mesh):
    placed = (P(("groups", "docs"), "proj"), P(("groups", "docs"), "proj"))
    return jax.shard_map(
        per_device,
        mesh=mesh,
        in_specs=placed,
        out_specs=P("proj", ("groups", "docs")),
        check_vma=False,
    )
```

```python
import jax
import jax.numpy as jnp
from jax import lax
from jax.sharding import PartitionSpec as P

WINDOW = 4
LINE = 4


def from_behind(value, axis, steps):
    count = lax.axis_size(axis)
    pairs = [(source, (source + steps) % count) for source in range(count)]
    return lax.ppermute(value, axis, pairs)


def products(rows, docs):
    return lax.dot_general(
        rows, docs, (((1,), (1,)), ((), ())), preferred_element_type=jnp.float32
    )


def ring(queries, store):
    blocks = [queries]
    for _ in range(WINDOW - 1):
        blocks.append(from_behind(blocks[-1], "docs", -1))
    return lax.psum_scatter(
        products(jnp.concatenate(blocks, axis=0), store),
        "proj",
        scatter_dimension=0,
        tiled=True,
    )


def after(value, *others):
    return lax.optimization_barrier((value,) + others)[0]


ENDS = [(0, 1), (1, 0), (2, 3), (3, 2)]
MIDDLE = [(1, 2), (2, 1)]
OUTWARD = [(1, 0), (2, 3)]
INWARD = [(0, 1), (3, 2)]
CORES = [(0, 1), (1, 0), (2, 3), (3, 2)]
CHIPS = [(0, 2), (1, 3), (2, 0), (3, 1)]


def along(value, pairs):
    return lax.ppermute(value, "docs", pairs)


def across(value, pairs):
    parts = lax.axis_size("proj")
    return lax.ppermute(
        value, ("docs", "proj"), [(a * parts + b, c * parts + d) for a, b, c, d in pairs]
    )


def line(queries, store):
    depth = queries.shape[1]
    cut = depth * 11 // 32 // 128 * 128
    last = depth * 29 // 32 // 128 * 128 - cut
    body, tail = slice(0, last), slice(last, None)
    place = lax.axis_index("docs")
    share = lax.axis_index("proj")
    inner = (place == 1) | (place == 2)
    left = place < 2
    even = share % 2 == 0
    low = share < 2
    near_store, far_store = store[:, :cut], store[:, cut:]

    middle = along(queries, MIDDLE)
    ends_near = along(queries[:, :cut], ENDS)
    ends_rest = along(after(queries[:, cut:], ends_near, far_store), ENDS)
    far_near = along(ends_near, MIDDLE)
    relayed = along(middle[:, :cut], OUTWARD)
    outer_store = along(after(far_store, middle), INWARD)
    far_body = along(after(ends_rest[:, body], middle), MIDDLE)
    far_relayed = along(after(far_near, relayed), OUTWARD)
    far_tail = along(after(ends_rest[:, tail], far_relayed), MIDDLE)

    own_part = products(queries, store)
    ends_part = products(ends_near, near_store) + products(ends_rest, far_store)
    middle_part = products(middle, store) + products(relayed, near_store)
    zeros = jnp.zeros_like(own_part)
    second = jnp.where(inner & left, middle_part, jnp.where(inner | left, ends_part, zeros))
    third = jnp.where(inner, zeros, middle_part)
    fourth = jnp.where(left, jnp.where(inner, ends_part, zeros), jnp.where(inner, middle_part, ends_part))
    kept = jnp.concatenate([jnp.where(even, own_part, second), jnp.where(even, third, fourth)], axis=0)
    given = jnp.concatenate([jnp.where(even, second, own_part), jnp.where(even, fourth, third)], axis=0)
    kept = kept + lax.ppermute(given, "proj", CORES)
    rows = queries.shape[0]
    early = jnp.where(low, kept[:rows], kept[rows:]) + lax.ppermute(
        jnp.where(low, kept[rows:], kept[:rows]), "proj", CHIPS
    )

    helped = products(middle[:, cut:], outer_store) + products(far_relayed, near_store)
    helped = helped + across(
        helped,
        [(z, p + odd, z, p + 1 - odd) for z, odd in [(0, 0), (1, 1), (2, 1), (3, 0)] for p in (0, 2)],
    )
    helped_one = across(helped, [(1, 0, 0, 2), (2, 0, 3, 2), (0, 1, 0, 3), (3, 3, 3, 1)])
    helped_two = across(helped, [(1, 2, 0, 2), (2, 2, 3, 2)])
    helped_stays = jnp.where(~inner & (share == jnp.where(left, 3, 1)), helped, 0.0)
    early = early + helped_one + helped_two + helped_stays

    far_part = products(far_near, near_store)
    kept_store = jnp.where(even, far_store[:, tail], outer_store[:, tail])
    given_store = jnp.where(even, outer_store[:, tail], far_store[:, tail])
    far_body, far_part, kept_store, given_store, helped = lax.optimization_barrier(
        (far_body, far_part, kept_store, given_store, helped)
    )
    far_part = far_part + products(far_body, far_store[:, body])
    outer_part = products(far_body, outer_store[:, body])
    kept = jnp.where(even, far_part, outer_part)
    given = jnp.where(even, outer_part, far_part)
    kept, given, kept_store, given_store, early = lax.optimization_barrier(
        (kept, given, kept_store, given_store, early)
    )
    given = given + products(far_tail, given_store)
    kept = kept + products(far_tail, kept_store)
    kept = kept + lax.ppermute(given, "proj", CORES)
    two = across(kept, [(1, 3, 0, 3), (2, 1, 3, 1)])
    one = across(kept, [(1, 0, 1, 2), (2, 0, 2, 2), (1, 1, 0, 3), (2, 3, 3, 1)])
    return early + jnp.where(inner & (share == 2), kept, 0.0) + two + one


def per_device(queries, store):
    if lax.axis_size("docs") == LINE and lax.axis_size("proj") == WINDOW:
        return line(queries, store)
    return ring(queries, store)


def solution(mesh):
    placed = (P(("groups", "docs"), "proj"), P(("groups", "docs"), "proj"))
    return jax.shard_map(
        per_device,
        mesh=mesh,
        in_specs=placed,
        out_specs=P("proj", ("groups", "docs")),
        check_vma=False,
    )
```
